32 devices in a mesh: outer: 8 (over y, x, core), inner: 4 (over z).
Axes of the slice: x: 2, y: 2, z: 4, core: 2. Of those that a mesh axis runs over, the one named last changes fastest.
Arguments:
- query_proj: bfloat16 [49152, 2048], P(('outer', 'inner')), may hold values from -6 to 6
- key_proj: bfloat16 [49152, 2048], P(('outer', 'inner')), may hold values from -6 to 6
- value_proj: bfloat16 [49152, 2048], P(('outer', 'inner')), may hold values from -6 to 6
- norm_gain: float32 [2048], replicated, may hold values from 0.25 to 1.75
Outputs:
- attended: bfloat16 [49152, 2048], P(('outer', 'inner'))
The draws below stay inside these ranges and needn't reach their ends.
All inputs are finite; a program needn't handle non-finite values.
Results may differ from the reference program's by a relative error of at most 0.0049.
Values sent between devices are 32-bit elements; how exact they have to be, the bound alone decides.
A program may use at most 192 MiB of HBM per device.

```python
import jax
import jax.numpy as jnp
from jax import lax

H = 16
DK = 128
SPAN = 256
SEQ = 49152
HD = 2048


def block_levels(key, shape, shards, low, top_value):
    level = 1.0
    for position, blocks in shards:
        heights = jax.random.uniform(jax.random.fold_in(jax.random.fold_in(key, 6), position), (blocks,), jnp.float32, low / len(shards), top_value / len(shards))
        level = level * jnp.repeat(jnp.exp(heights), shape[position] // blocks).reshape((-1,) + (1,) * (len(shape) - 1 - position))
    return level


def noise(stream_key, shape, scale, bound, shards=(), dtype=jnp.bfloat16):
    array = scale * jax.random.normal(stream_key, shape, jnp.float32)
    if shards:
        array = array * block_levels(stream_key, shape, shards, -0.22, 0.18)
    return jnp.clip(array, -bound, bound).astype(dtype)


def setup_inputs(seed: int = 0) -> dict:
    keys = jax.random.split(jax.random.key(seed), 5)
    return {
        "query_proj": noise(keys[0], (SEQ, HD), 1.0, 6.0, ((0, 32),)),
        "key_proj": noise(keys[1], (SEQ, HD), 1.0, 6.0, ((0, 32),)),
        "value_proj": noise(keys[2], (SEQ, HD), 1.0, 6.0, ((0, 32),)),
        "norm_gain": jnp.clip(1.0 + 0.15 * jax.random.normal(keys[3], (HD,), jnp.float32), 0.25, 1.75),
    }


def reference(query_proj, key_proj, value_proj, norm_gain):
    count = SEQ // SPAN
    shape = (count, SPAN, H, DK)
    queries = query_proj.reshape(shape)
    keys_all = key_proj.reshape(shape)
    values_all = value_proj.reshape(shape)
    rows = jnp.arange(SPAN)
    causal = rows[:, None] >= rows[None, :]
    gain = norm_gain.reshape(H, DK)

    def step(state, blocks):
        query_block, key_block, value_block = blocks
        qfloat = query_block.astype(jnp.float32)
        kfloat = key_block.astype(jnp.float32)
        vfloat = value_block.astype(jnp.float32)
        rounded = lax.optimization_barrier(state.astype(jnp.bfloat16)).astype(jnp.float32)
        carried = jnp.einsum('chd,hde->che', qfloat, rounded)
        scores = jnp.einsum('chd,shd->hcs', qfloat, kfloat)
        scores = jnp.where(causal[None], scores, 0.0)
        scores = lax.optimization_barrier(scores.astype(jnp.bfloat16)).astype(jnp.float32)
        local = jnp.einsum('hcs,she->che', scores, vfloat)
        raw = carried + local
        state = state + jnp.einsum('chd,che->hde', kfloat, vfloat)
        meansq = lax.optimization_barrier(jnp.mean(raw * raw, axis=-1, keepdims=True))
        normed = raw * lax.rsqrt(meansq + 1e-06) * gain
        return (state, normed.astype(jnp.bfloat16).reshape(SPAN, H * DK))
    start = jnp.zeros((H, DK, DK), jnp.float32)
    _, outputs = lax.scan(step, start, (queries, keys_all, values_all))
    return outputs.reshape(SEQ, H * DK)
```

```python
import functools

import jax
import jax.numpy as jnp
from jax import lax
from jax.experimental import pallas as pl
from jax.experimental.pallas import tpu as pltpu
from jax.sharding import PartitionSpec as P

DK = 128
SPAN = 256
HOP = 2
LOCAL = 4
MESH = pl.DeviceIdType.MESH
F32 = jnp.float32
BF16 = jnp.bfloat16


def dot(a, b, ca, cb):
    return lax.dot_general(a, b, (((ca,), (cb,)), ((), ())), preferred_element_type=F32)


def kernel(
    n_outer, n_inner, heads, count, steps,
    q_hbm, k_hbm, v_hbm, g_ref, o_hbm,
    qb, kb, vb, run, loc, fr, br, fs, bs, xs, xr,
    in_sem, out_sem, f_ss, f_rs, b_ss, b_rs, x_ss, x_rs,
):
    o = lax.axis_index("outer")
    z = lax.axis_index("inner")
    last = n_inner - 1

    def fetch(j, src, dst, h):
        return pltpu.make_async_copy(
            src.at[:, pl.ds(pl.multiple_of(h * DK, DK), DK)], dst.at[h], in_sem.at[j, h]
        )

    def store(h):
        return pltpu.make_async_copy(
            qb.at[h], o_hbm.at[:, pl.ds(pl.multiple_of(h * DK, DK), DK)], out_sem.at[h]
        )

    def forward(h):
        return pltpu.make_async_remote_copy(
            src_ref=fs.at[h], dst_ref=fr.at[h], send_sem=f_ss.at[h], recv_sem=f_rs.at[h],
            device_id=(o, lax.rem(z + 1, n_inner)), device_id_type=MESH,
        )

    def backward(h):
        return pltpu.make_async_remote_copy(
            src_ref=bs.at[h], dst_ref=br.at[h], send_sem=b_ss.at[h], recv_sem=b_rs.at[h],
            device_id=(o, lax.rem(z + last, n_inner)), device_id_type=MESH,
        )

    bits = [lax.rem(o // (1 << k), 2) for k in range(steps)]
    partners = [o + (1 - 2 * bits[k]) * (1 << k) for k in range(steps)]

    def across(k, h):
        return pltpu.make_async_remote_copy(
            src_ref=xs.at[k, h], dst_ref=xr.at[k, h], send_sem=x_ss.at[k, h], recv_sem=x_rs.at[k, h],
            device_id=(partners[k], z), device_id_type=MESH,
        )

    def load_states(h, c):
        fetch(1, k_hbm, kb, h).start()
        fetch(2, v_hbm, vb, h).start()
        return c

    def load_queries(h, c):
        fetch(0, q_hbm, qb, h).start()
        return c

    lax.fori_loop(0, heads, load_states, 0)
    lax.fori_loop(0, heads, load_queries, 0)

    barrier = pltpu.get_barrier_semaphore()
    for k in range(steps):
        pl.semaphore_signal(barrier, inc=1, device_id=(partners[k], z), device_id_type=MESH)

    @pl.when(z > 0)
    def _():
        pl.semaphore_signal(barrier, inc=1, device_id=(o, z - 1), device_id_type=MESH)

    @pl.when(z < last)
    def _():
        pl.semaphore_signal(barrier, inc=1, device_id=(o, z + 1), device_id_type=MESH)

    pl.semaphore_wait(barrier, steps + jnp.minimum(z, 1) + jnp.minimum(last - z, 1))

    def at(t, lag, body):
        h = t - lag

        @pl.when((h >= 0) & (h < heads))
        def _():
            body(h)

    def rows(n):
        return pl.ds(n * SPAN, SPAN)

    def states(h):
        fetch(1, k_hbm, kb, h).wait()
        fetch(2, v_hbm, vb, h).wait()
        total = None
        for n in range(count):
            new = dot(kb[h, rows(n), :], vb[h, rows(n), :], 0, 0)
            total = new if total is None else total + new
            run[h, n] = total

    def go_forward(h):
        @pl.when(z == 0)
        def _():
            fr[h] = jnp.zeros((DK, DK), F32)

        @pl.when(z > 0)
        def _():
            forward(h).wait_recv()

        @pl.when(z < last)
        def _():
            fs[h] = fr[h] + run[h, count - 1]
            forward(h).start()

    def go_backward(h):
        @pl.when(z == last)
        def _():
            br[h] = jnp.zeros((DK, DK), F32)

        @pl.when(z < last)
        def _():
            backward(h).wait_recv()

        @pl.when(z > 0)
        def _():
            bs[h] = br[h] + run[h, count - 1]
            backward(h).start()

    def exchange(k, h):
        if k == 0:
            total = fr[h] + run[h, count - 1] + br[h]
        else:
            total = receive(k - 1, h)
        if k < steps - 1:
            xs[k, h] = total
            across(k, h).start()
        elif k == steps - 1:

            @pl.when(bits[k] == 0)
            def _():
                xs[k, h] = total
                across(k, h).start()

    def receive(k, h):
        across(k, h).wait_recv()
        came = xr[k, h]

        @pl.when(bits[k] == 1)
        def _():
            fr[h] = fr[h] + came

        return xs[k, h] + came

    def local(h):
        fetch(0, q_hbm, qb, h).wait()
        causal = lax.broadcasted_iota(jnp.int32, (SPAN, SPAN), 0) >= lax.broadcasted_iota(
            jnp.int32, (SPAN, SPAN), 1
        )
        for n in range(count):
            scores = dot(qb[h, rows(n), :], kb[h, rows(n), :], 1, 1)
            scores = jnp.where(causal, scores, 0.0).astype(BF16)
            loc[h, rows(n), :] = dot(scores, vb[h, rows(n), :], 1, 0)

    def finish(h):
        if steps:

            @pl.when(bits[steps - 1] == 1)
            def _():
                across(steps - 1, h).wait_recv()
                fr[h] = fr[h] + xr[steps - 1, h]

        gain = g_ref[pl.ds(h, 1), :]
        prefix = fr[h]
        for n in range(count):
            carried = prefix if n == 0 else prefix + run[h, n - 1]
            raw = dot(qb[h, rows(n), :], carried.astype(BF16), 1, 0) + loc[h, rows(n), :]
            meansq = jnp.mean(raw * raw, axis=-1, keepdims=True)
            qb[h, rows(n), :] = (raw * lax.rsqrt(meansq + 1e-06) * gain).astype(BF16)
        store(h).start()

    base = HOP * last

    def step(t, c):
        at(t, 0, states)
        at(t, HOP * z, go_forward)
        at(t, HOP * (last - z), go_backward)
        for k in range(steps):
            at(t, base + HOP * k, functools.partial(exchange, k))
        at(t, LOCAL, local)
        at(t, base + HOP * steps, finish)
        return c

    lax.fori_loop(0, heads + base + HOP * steps, step, 0)

    def drain(h, c):
        store(h).wait()

        @pl.when(z < last)
        def _():
            forward(h).wait_send()

        @pl.when(z > 0)
        def _():
            backward(h).wait_send()

        for k in range(steps - 1):
            across(k, h).wait_send()
        if steps:

            @pl.when(bits[steps - 1] == 0)
            def _():
                across(steps - 1, h).wait_send()

        return c

    lax.fori_loop(0, heads, drain, 0)


def solution(mesh):
    n_outer, n_inner = mesh.shape["outer"], mesh.shape["inner"]
    steps = n_outer.bit_length() - 1
    assert n_outer == 1 << steps

    def shards(query, key, value, gain):
        tokens, width = query.shape
        heads, count = width // DK, tokens // SPAN
        dma = pltpu.SemaphoreType.DMA
        some = max(steps, 1)
        state = (heads, DK, DK)
        return pl.pallas_call(
            functools.partial(kernel, n_outer, n_inner, heads, count, steps),
            out_shape=jax.ShapeDtypeStruct((tokens, width), BF16),
            in_specs=[pl.BlockSpec(memory_space=pl.ANY)] * 3
            + [pl.BlockSpec(memory_space=pltpu.VMEM)],
            out_specs=pl.BlockSpec(memory_space=pl.ANY),
            scratch_shapes=[
                pltpu.VMEM((heads, tokens, DK), BF16),
                pltpu.VMEM((heads, tokens, DK), BF16),
                pltpu.VMEM((heads, tokens, DK), BF16),
                pltpu.VMEM((heads, count, DK, DK), F32),
                pltpu.VMEM((heads, tokens, DK), F32),
                pltpu.VMEM(state, F32),
                pltpu.VMEM(state, F32),
                pltpu.VMEM(state, F32),
                pltpu.VMEM(state, F32),
                pltpu.VMEM((some,) + state, F32),
                pltpu.VMEM((some,) + state, F32),
                dma((3, heads)),
                dma((heads,)),
                dma((heads,)),
                dma((heads,)),
                dma((heads,)),
                dma((heads,)),
                dma((some, heads)),
                dma((some, heads)),
            ],
            compiler_params=pltpu.CompilerParams(
                collective_id=0, has_side_effects=True, vmem_limit_bytes=60 * 1024 * 1024
            ),
        )(query, key, value, gain.reshape(heads, DK))

    return jax.shard_map(
        shards,
        mesh=mesh,
        in_specs=(
            P(("outer", "inner"), None),
            P(("outer", "inner"), None),
            P(("outer", "inner"), None),
            P(),
        ),
        out_specs=P(("outer", "inner"), None),
        check_vma=False,
    )
```

```python
import functools

import jax
import jax.numpy as jnp
from jax import lax
from jax.experimental import pallas as pl
from jax.experimental.pallas import tpu as pltpu
from jax.sharding import PartitionSpec as P

DK = 128
SPAN = 256
HOP = 3
NEAR = 2
FAR = 3
LOCAL = 4
MESH = pl.DeviceIdType.MESH
F32 = jnp.float32
BF16 = jnp.bfloat16


def dot(a, b, ca, cb):
    return lax.dot_general(a, b, (((ca,), (cb,)), ((), ())), preferred_element_type=F32)


def kernel(
    n_outer, n_inner, heads, count, steps,
    q_hbm, k_hbm, v_hbm, g_hbm, o_hbm,
    g_ref, g_sem, qb, kb, vb, run, loc, fr, br, fs, bs, xs, xr,
    in_sem, out_sem, f_ss, f_rs, b_ss, b_rs, x_ss, x_rs,
):
    o = lax.axis_index("outer")
    z = lax.axis_index("inner")
    last = n_inner - 1

    def fetch(j, src, dst, h):
        return pltpu.make_async_copy(
            src.at[:, pl.ds(pl.multiple_of(h * DK, DK), DK)], dst.at[h], in_sem.at[j, h]
        )

    def store(h):
        return pltpu.make_async_copy(
            qb.at[h], o_hbm.at[:, pl.ds(pl.multiple_of(h * DK, DK), DK)], out_sem.at[h]
        )

    def forward(h):
        return pltpu.make_async_remote_copy(
            src_ref=fs.at[h], dst_ref=fr.at[h], send_sem=f_ss.at[h], recv_sem=f_rs.at[h],
            device_id=(o, lax.rem(z + 1, n_inner)), device_id_type=MESH,
        )

    def backward(h):
        return pltpu.make_async_remote_copy(
            src_ref=bs.at[h], dst_ref=br.at[h], send_sem=b_ss.at[h], recv_sem=b_rs.at[h],
            device_id=(o, lax.rem(z + last, n_inner)), device_id_type=MESH,
        )

    bits = [lax.rem(o // (1 << k), 2) for k in range(steps)]
    partners = [o + (1 - 2 * bits[k]) * (1 << k) for k in range(steps)]

    def across(k, h):
        return pltpu.make_async_remote_copy(
            src_ref=xs.at[k, h], dst_ref=xr.at[k, h], send_sem=x_ss.at[k, h], recv_sem=x_rs.at[k, h],
            device_id=(partners[k], z), device_id_type=MESH,
        )

    def load_states(h, c):
        fetch(1, k_hbm, kb, h).start()
        fetch(2, v_hbm, vb, h).start()
        return c

    def load_queries(h, c):
        fetch(0, q_hbm, qb, h).start()
        return c

    lax.fori_loop(0, heads, load_states, 0)
    lax.fori_loop(0, heads, load_queries, 0)
    gains = pltpu.make_async_copy(g_hbm, g_ref, g_sem)
    gains.start()

    barrier = pltpu.get_barrier_semaphore()
    for k in range(steps):
        pl.semaphore_signal(barrier, inc=1, device_id=(partners[k], z), device_id_type=MESH)

    @pl.when(z > 0)
    def _():
        pl.semaphore_signal(barrier, inc=1, device_id=(o, z - 1), device_id_type=MESH)

    @pl.when(z < last)
    def _():
        pl.semaphore_signal(barrier, inc=1, device_id=(o, z + 1), device_id_type=MESH)

    pl.semaphore_wait(barrier, steps + jnp.minimum(z, 1) + jnp.minimum(last - z, 1))

    def at(t, lag, body):
        h = t - lag

        @pl.when((h >= 0) & (h < heads))
        def _():
            body(h)

    def rows(n):
        return pl.ds(n * SPAN, SPAN)

    def states(h):
        fetch(1, k_hbm, kb, h).wait()
        fetch(2, v_hbm, vb, h).wait()
        total = None
        for n in range(count):
            new = dot(kb[h, rows(n), :], vb[h, rows(n), :], 0, 0)
            total = new if total is None else total + new
            run[h, n] = total

    def go_forward(h):
        @pl.when(z == 0)
        def _():
            fr[h] = jnp.zeros((DK, DK), F32)

        @pl.when(z > 0)
        def _():
            forward(h).wait_recv()

        @pl.when(z < last)
        def _():
            fs[h] = fr[h] + run[h, count - 1]
            forward(h).start()

    def go_backward(h):
        @pl.when(z == last)
        def _():
            br[h] = jnp.zeros((DK, DK), F32)

        @pl.when(z < last)
        def _():
            backward(h).wait_recv()

        @pl.when(z > 0)
        def _():
            bs[h] = br[h] + run[h, count - 1]
            backward(h).start()

    def exchange(k, h):
        if k == 0:
            total = fr[h] + run[h, count - 1] + br[h]
        else:
            total = receive(k - 1, h)
        if k < steps - 1:
            xs[k, h] = total
            across(k, h).start()
        elif k == steps - 1:

            @pl.when(bits[k] == 0)
            def _():
                xs[k, h] = total
                across(k, h).start()

    def receive(k, h):
        across(k, h).wait_recv()
        came = xr[k, h]

        @pl.when(bits[k] == 1)
        def _():
            fr[h] = fr[h] + came

        return xs[k, h] + came

    def local(h):
        fetch(0, q_hbm, qb, h).wait()
        causal = lax.broadcasted_iota(jnp.int32, (SPAN, SPAN), 0) >= lax.broadcasted_iota(
            jnp.int32, (SPAN, SPAN), 1
        )
        for n in range(count):
            scores = dot(qb[h, rows(n), :], kb[h, rows(n), :], 1, 1)
            scores = jnp.where(causal, scores, 0.0).astype(BF16)
            loc[h, rows(n), :] = dot(scores, vb[h, rows(n), :], 1, 0)

    def finish(h):
        if steps:

            @pl.when(bits[steps - 1] == 1)
            def _():
                across(steps - 1, h).wait_recv()
                fr[h] = fr[h] + xr[steps - 1, h]

        gain = g_ref[pl.ds(h, 1), :]
        prefix = fr[h]
        for n in range(count):
            carried = prefix if n == 0 else prefix + run[h, n - 1]
            raw = dot(qb[h, rows(n), :], carried.astype(BF16), 1, 0) + loc[h, rows(n), :]
            meansq = jnp.mean(raw * raw, axis=-1, keepdims=True)
            qb[h, rows(n), :] = (raw * lax.rsqrt(meansq + 1e-06) * gain).astype(BF16)
        store(h).start()

    gains.wait()
    base = HOP * last
    lags = [0] + [NEAR + FAR * k for k in range(steps)]

    def step(t, c):
        at(t, 0, states)
        at(t, HOP * z, go_forward)
        at(t, HOP * (last - z), go_backward)
        for k in range(steps):
            at(t, base + lags[k], functools.partial(exchange, k))
        at(t, LOCAL, local)
        at(t, base + lags[steps], finish)
        return c

    lax.fori_loop(0, heads + base + lags[steps], step, 0)

    def drain(h, c):
        store(h).wait()

        @pl.when(z < last)
        def _():
            forward(h).wait_send()

        @pl.when(z > 0)
        def _():
            backward(h).wait_send()

        for k in range(steps - 1):
            across(k, h).wait_send()
        if steps:

            @pl.when(bits[steps - 1] == 0)
            def _():
                across(steps - 1, h).wait_send()

        return c

    lax.fori_loop(0, heads, drain, 0)


def solution(mesh):
    n_outer, n_inner = mesh.shape["outer"], mesh.shape["inner"]
    steps = n_outer.bit_length() - 1
    assert n_outer == 1 << steps

    def shards(query, key, value, gain):
        tokens, width = query.shape
        heads, count = width // DK, tokens // SPAN
        dma = pltpu.SemaphoreType.DMA
        some = max(steps, 1)
        state = (heads, DK, DK)
        return pl.pallas_call(
            functools.partial(kernel, n_outer, n_inner, heads, count, steps),
            out_shape=jax.ShapeDtypeStruct((tokens, width), BF16),
            in_specs=[pl.BlockSpec(memory_space=pl.ANY)] * 4,
            out_specs=pl.BlockSpec(memory_space=pl.ANY),
            scratch_shapes=[
                pltpu.VMEM((heads, DK), F32),
                dma,
                pltpu.VMEM((heads, tokens, DK), BF16),
                pltpu.VMEM((heads, tokens, DK), BF16),
                pltpu.VMEM((heads, tokens, DK), BF16),
                pltpu.VMEM((heads, count, DK, DK), F32),
                pltpu.VMEM((heads, tokens, DK), F32),
                pltpu.VMEM(state, F32),
                pltpu.VMEM(state, F32),
                pltpu.VMEM(state, F32),
                pltpu.VMEM(state, F32),
                pltpu.VMEM((some,) + state, F32),
                pltpu.VMEM((some,) + state, F32),
                dma((3, heads)),
                dma((heads,)),
                dma((heads,)),
                dma((heads,)),
                dma((heads,)),
                dma((heads,)),
                dma((some, heads)),
                dma((some, heads)),
            ],
            compiler_params=pltpu.CompilerParams(
                collective_id=0, has_side_effects=True, vmem_limit_bytes=(41 + 2 * some) * 1024 * 1024
            ),
        )(query, key, value, gain.reshape(heads, DK))

    return jax.shard_map(
        shards,
        mesh=mesh,
        in_specs=(
            P(("outer", "inner"), None),
            P(("outer", "inner"), None),
            P(("outer", "inner"), None),
            P(),
        ),
        out_specs=P(("outer", "inner"), None),
        check_vma=False,
    )
```

```python
import functools

import jax
import jax.numpy as jnp
from jax import lax
from jax.experimental import pallas as pl
from jax.experimental.pallas import tpu as pltpu
from jax.sharding import PartitionSpec as P

DK = 128
SPAN = 256
HOP = 3
NEAR = 2
FAR = 3
LOCAL = 4
MESH = pl.DeviceIdType.MESH
F32 = jnp.float32
BF16 = jnp.bfloat16


def dot(a, b, ca, cb):
    return lax.dot_general(a, b, (((ca,), (cb,)), ((), ())), preferred_element_type=F32)


def kernel(
    n_outer, n_inner, heads, count, steps,
    q_hbm, k_hbm, v_hbm, g_hbm, o_hbm,
    g_ref, g_sem, ex, qb, kb, vb, run, loc, fr, br, fs, bs, xs, xr,
    in_sem, out_sem, f_ss, f_rs, b_ss, b_rs, x_ss, x_rs,
):
    o = lax.axis_index("outer")
    z = lax.axis_index("inner")
    last = n_inner - 1
    half = heads // 2

    def fetch(j, src, dst, h):
        return pltpu.make_async_copy(
            src.at[:, pl.ds(pl.multiple_of(h * DK, DK), DK)], dst.at[h], in_sem.at[j, h]
        )

    def store(h):
        return pltpu.make_async_copy(
            qb.at[h], o_hbm.at[:, pl.ds(pl.multiple_of(h * DK, DK), DK)], out_sem.at[h]
        )

    def forward(h):
        return pltpu.make_async_remote_copy(
            src_ref=fs.at[h], dst_ref=fr.at[h], send_sem=f_ss.at[h], recv_sem=f_rs.at[h],
            device_id=(o, lax.rem(z + 1, n_inner)), device_id_type=MESH,
        )

    def backward(h):
        return pltpu.make_async_remote_copy(
            src_ref=bs.at[h], dst_ref=br.at[h], send_sem=b_ss.at[h], recv_sem=b_rs.at[h],
            device_id=(o, lax.rem(z + last, n_inner)), device_id_type=MESH,
        )

    bits = [lax.rem(o // (1 << k), 2) for k in range(steps)]
    partners = [o + (1 - 2 * bits[k]) * (1 << k) for k in range(steps)]

    def across(k, h):
        return pltpu.make_async_remote_copy(
            src_ref=xs.at[k, h], dst_ref=xr.at[k, h], send_sem=x_ss.at[k, h], recv_sem=x_rs.at[k, h],
            device_id=(partners[k], z), device_id_type=MESH,
        )

    def load_states(h, c):
        for g in (h, h + half):
            fetch(1, k_hbm, kb, g).start()
            fetch(2, v_hbm, vb, g).start()
        return c

    def load_queries(h, c):
        fetch(0, q_hbm, qb, h).start()
        return c

    lax.fori_loop(0, half, load_states, 0)
    lax.fori_loop(0, heads, load_queries, 0)
    gains = pltpu.make_async_copy(g_hbm, g_ref, g_sem)
    gains.start()

    barrier = pltpu.get_barrier_semaphore()
    for k in range(steps):
        pl.semaphore_signal(barrier, inc=1, device_id=(partners[k], z), device_id_type=MESH)

    @pl.when(z > 0)
    def _():
        pl.semaphore_signal(barrier, inc=1, device_id=(o, z - 1), device_id_type=MESH)

    @pl.when(z < last)
    def _():
        pl.semaphore_signal(barrier, inc=1, device_id=(o, z + 1), device_id_type=MESH)

    pl.semaphore_wait(barrier, steps + jnp.minimum(z, 1) + jnp.minimum(last - z, 1))

    def at(t, lag, body, first=0, number=half):
        h = t - lag

        @pl.when((h >= 0) & (h < number))
        def _():
            body(h + first)

    def rows(n):
        return pl.ds(n * SPAN, SPAN)

    def states(h):
        fetch(1, k_hbm, kb, h).wait()
        fetch(2, v_hbm, vb, h).wait()
        total = None
        for n in range(count):
            new = dot(kb[h, rows(n), :], vb[h, rows(n), :], 0, 0)
            total = new if total is None else total + new
            run[h, n] = total

    def go_forward(early, h):
        @pl.when(z == 0)
        def _():
            fr[h] = jnp.zeros((DK, DK), F32)

        @pl.when(z > 0)
        def _():
            forward(h).wait_recv()

        @pl.when(z < last)
        def _():
            mine = run[h, count - 1]
            fs[h] = fr[h] + (mine if early else mine + ex[h - half])
            forward(h).start()

    def go_backward(early, h):
        @pl.when(z == last)
        def _():
            br[h] = jnp.zeros((DK, DK), F32)

        @pl.when(z < last)
        def _():
            backward(h).wait_recv()

        @pl.when(z > 0)
        def _():
            bs[h] = br[h] + (run[h, count - 1] if early else ex[h - half])
            backward(h).start()

    def exchange(early, k, h):
        if k > 0:
            total = receive(early, k - 1, h)
        elif early:
            total = fr[h] + run[h, count - 1] + br[h]
        else:
            total = run[h, count - 1]
            ex[h - half] = jnp.zeros((DK, DK), F32)
        if k < steps - 1:
            xs[k, h] = total
            across(k, h).start()
        else:

            @pl.when(bits[k] == 0)
            def _():
                xs[k, h] = total
                across(k, h).start()

    def add(early, h, came):
        if early:
            fr[h] = fr[h] + came
        else:
            ex[h - half] = ex[h - half] + came

    def receive(early, k, h):
        across(k, h).wait_recv()
        came = xr[k, h]

        @pl.when(bits[k] == 1)
        def _():
            add(early, h, came)

        return xs[k, h] + came

    def settle(early, h):
        if steps == 0:
            if not early:
                ex[h - half] = jnp.zeros((DK, DK), F32)
            return

        @pl.when(bits[steps - 1] == 1)
        def _():
            across(steps - 1, h).wait_recv()
            add(early, h, xr[steps - 1, h])

    def local(h):
        fetch(0, q_hbm, qb, h).wait()
        causal = lax.broadcasted_iota(jnp.int32, (SPAN, SPAN), 0) >= lax.broadcasted_iota(
            jnp.int32, (SPAN, SPAN), 1
        )
        for n in range(count):
            scores = dot(qb[h, rows(n), :], kb[h, rows(n), :], 1, 1)
            scores = jnp.where(causal, scores, 0.0).astype(BF16)
            loc[h, rows(n), :] = dot(scores, vb[h, rows(n), :], 1, 0)

    def finish(early, h):
        if early:
            settle(early, h)
        else:
            fr[h] = fr[h] + ex[h - half] + br[h]
        gain = g_ref[pl.ds(h, 1), :]
        prefix = fr[h]
        for n in range(count):
            carried = prefix if n == 0 else prefix + run[h, n - 1]
            raw = dot(qb[h, rows(n), :], carried.astype(BF16), 1, 0) + loc[h, rows(n), :]
            meansq = jnp.mean(raw * raw, axis=-1, keepdims=True)
            qb[h, rows(n), :] = (raw * lax.rsqrt(meansq + 1e-06) * gain).astype(BF16)
        store(h).start()

    gains.wait()
    base = HOP * last
    lags = [0] + [NEAR + FAR * k for k in range(steps)]

    bind = functools.partial

    def step(t, c):
        at(t, 0, states)
        at(t, 0, states, half)
        at(t, HOP * z, bind(go_forward, True))
        at(t, HOP * (last - z), bind(go_backward, True))
        for k in range(steps):
            at(t, lags[k], bind(exchange, False, k), half)
        at(t, lags[steps], bind(settle, False), half)
        at(t, lags[steps] + HOP * z, bind(go_forward, False), half)
        at(t, lags[steps] + HOP * (last - z), bind(go_backward, False), half)
        for k in range(steps):
            at(t, base + lags[k], bind(exchange, True, k))
        at(t, LOCAL, local, 0, heads)
        at(t, base + lags[steps], bind(finish, True))
        at(t, base + lags[steps], bind(finish, False), half)
        return c

    lax.fori_loop(0, half + max(base + lags[steps], half + LOCAL), step, 0)

    def drain(h, c):
        store(h).wait()

        @pl.when(z < last)
        def _():
            forward(h).wait_send()

        @pl.when(z > 0)
        def _():
            backward(h).wait_send()

        for k in range(steps - 1):
            across(k, h).wait_send()
        if steps:

            @pl.when(bits[steps - 1] == 0)
            def _():
                across(steps - 1, h).wait_send()

        return c

    lax.fori_loop(0, heads, drain, 0)


def solution(mesh):
    n_outer, n_inner = mesh.shape["outer"], mesh.shape["inner"]
    steps = n_outer.bit_length() - 1
    assert n_outer == 1 << steps

    def shards(query, key, value, gain):
        tokens, width = query.shape
        heads, count = width // DK, tokens // SPAN
        dma = pltpu.SemaphoreType.DMA
        some = max(steps, 1)
        state = (heads, DK, DK)
        return pl.pallas_call(
            functools.partial(kernel, n_outer, n_inner, heads, count, steps),
            out_shape=jax.ShapeDtypeStruct((tokens, width), BF16),
            in_specs=[pl.BlockSpec(memory_space=pl.ANY)] * 4,
            out_specs=pl.BlockSpec(memory_space=pl.ANY),
            scratch_shapes=[
                pltpu.VMEM((heads, DK), F32),
                dma,
                pltpu.VMEM((heads // 2, DK, DK), F32),
                pltpu.VMEM((heads, tokens, DK), BF16),
                pltpu.VMEM((heads, tokens, DK), BF16),
                pltpu.VMEM((heads, tokens, DK), BF16),
                pltpu.VMEM((heads, count, DK, DK), F32),
                pltpu.VMEM((heads, tokens, DK), F32),
                pltpu.VMEM(state, F32),
                pltpu.VMEM(state, F32),
                pltpu.VMEM(state, F32),
                pltpu.VMEM(state, F32),
                pltpu.VMEM((some,) + state, F32),
                pltpu.VMEM((some,) + state, F32),
                dma((3, heads)),
                dma((heads,)),
                dma((heads,)),
                dma((heads,)),
                dma((heads,)),
                dma((heads,)),
                dma((some, heads)),
                dma((some, heads)),
            ],
            compiler_params=pltpu.CompilerParams(
                collective_id=0, has_side_effects=True, vmem_limit_bytes=(38 + 3 * some) * 1024 * 1024
            ),
        )(query, key, value, gain.reshape(heads, DK))

    return jax.shard_map(
        shards,
        mesh=mesh,
        in_specs=(
            P(("outer", "inner"), None),
            P(("outer", "inner"), None),
            P(("outer", "inner"), None),
            P(),
        ),
        out_specs=P(("outer", "inner"), None),
        check_vma=False,
    )
```
